32 devices in a mesh: gx: 8 (over y, x, core), gy: 4 (over z).
Axes of the slice: x: 2, y: 2, z: 4, core: 2. Of those that a mesh axis runs over, the one named last changes fastest.
Arguments:
- field_in: bfloat16 [32, 16, 1024], P('gx', 'gy'), may hold values from -6 to 6
- w_first: bfloat16 [27, 64, 64], replicated, may hold values from -0.15625 to 0.15625
- b_first: float32 [64], replicated, may hold values from -3 to 3
- w_upper: bfloat16 [8, 64, 64], replicated, may hold values from -0.75 to 0.75
- w_second: bfloat16 [27, 64, 64], replicated, may hold values from -0.15625 to 0.15625
- b_second: float32 [64], replicated, may hold values from -3 to 3
- cotangent: bfloat16 [64, 32, 2048], P('gx', 'gy'), may hold values from -6 to 6
- tile_weights: int32 [8, 4], P('gx', 'gy'), may hold values from 0 to 3
Outputs:
- output_field: bfloat16 [64, 32, 2048], P('gx', 'gy')
- grad_input: bfloat16 [32, 16, 1024], P('gx', 'gy')
- grad_first: float32 [27, 64, 64], replicated
- grad_upper: float32 [8, 64, 64], replicated
- grad_second: float32 [27, 64, 64], replicated
The draws below stay inside these ranges and needn't reach their ends.
All inputs are finite; a program needn't handle non-finite values.
Results may differ from the reference program's by a relative error of at most 0.01.
Values may be sent and summed in bfloat16 or wider, within the bound.
A program may use at most 64 MiB of HBM per device.

```python
import math
import jax
import jax.numpy as jnp
import numpy as np
from jax import lax

C = 64
NZ = 16
TT = 8
NX = 32
NY = 16


def place_ends(drawn, own_key, low, high):
    extent = drawn.shape
    index_at = [jax.random.randint(jax.random.fold_in(own_key, axis), (), 0, extent[axis]) for axis in range(len(extent))]
    drawn = drawn.at[tuple(index_at)].set(low)
    longest = extent.index(max(extent))
    index_at[longest] = (index_at[longest] + 1) % extent[longest]
    return drawn.at[tuple(index_at)].set(high)


def steps_of(own_key, shape, pieces, smallest, largest):
    gain = 1.0
    for position, blocks in pieces:
        draws = jax.random.uniform(jax.random.fold_in(jax.random.fold_in(own_key, 6), position), (blocks,), jnp.float32, smallest / len(pieces), largest / len(pieces))
        gain = gain * jnp.repeat(jnp.exp(draws), shape[position] // blocks).reshape((-1,) + (1,) * (len(shape) - 1 - position))
    return gain


def cumulative_ranks(count, lean):
    loads = [(1 << 20) // math.isqrt(grade ** lean) + 1 for grade in range(1, count + 1)]
    width = 1 + sum(loads) // (1 << 30)
    return np.cumsum(np.array([max(1, weight // width) for weight in loads]))


def skewed_ids(key, dims, amount, lean):
    table = cumulative_ranks(amount, lean)
    lot = jax.random.randint(jax.random.fold_in(key, 1), dims, 0, int(table[amount - 1]))
    rank = jnp.searchsorted(jnp.asarray(table, jnp.int32), lot, side="right")
    return jax.random.permutation(jax.random.fold_in(key, 2), amount)[rank].astype(jnp.int32)


def gaussian(key, extent, spread, most, pieces=(), dtype=jnp.bfloat16):
    drawn = jax.random.normal(key, extent, jnp.float32) * spread
    if len(pieces) > 0:
        drawn = steps_of(key, extent, pieces, -0.22, 0.18) * drawn
    return jnp.clip(drawn, min=-most, max=most).astype(dtype)


def setup_inputs(seed: int = 0) -> dict:
    key_list = jax.random.split(jax.random.key(seed), 9)
    return {
        "field_in": gaussian(key_list[0], (NX, NY, NZ * C), 1.0, 6.0, ((0, 8), (1, 4))),
        "w_first": gaussian(key_list[1], (27, C, C), (27 * C) ** -0.5, 0.15625),
        "b_first": gaussian(key_list[2], (C,), 0.5, 3.0, (), jnp.float32),
        "w_upper": gaussian(key_list[3], (8, C, C), C ** -0.5, 0.75),
        "w_second": gaussian(key_list[4], (27, C, C), (27 * C) ** -0.5, 0.15625),
        "b_second": gaussian(key_list[5], (C,), 0.5, 3.0, (), jnp.float32),
        "cotangent": gaussian(key_list[6], (2 * NX, 2 * NY, 2 * NZ * C), 1.0, 6.0, ((0, 8), (1, 4))),
        "tile_weights": place_ends(skewed_ids(key_list[7], (2 * NX // TT, 2 * NY // TT), 4, 2), jax.random.fold_in(key_list[7], 3), 0, 3).astype(jnp.int32),
    }


def act(v):
    return 0.2 * v + 0.8 * jax.nn.softplus(v)

def slope(v):
    return 0.2 + 0.8 * jax.nn.sigmoid(v)

def pad_whole(field):
    padded = jnp.pad(field, ((1, 1), (1, 1), (0, 0), (0, 0)), mode='wrap')
    return jnp.pad(padded, ((0, 0), (0, 0), (1, 1), (0, 0)))

def conv_whole(field, weights):
    rows, cols, depth, chans = field.shape
    padded = pad_whole(field)
    blk = math.gcd(rows, 16)

    def one_block(start):
        slab = lax.dynamic_slice_in_dim(padded, start, blk + 2, 0)
        total = jnp.zeros((blk * cols * depth, weights.shape[2]), jnp.float32)
        for k in range(27):
            ox, oy, oz = (k // 9, k // 3 % 3, k % 3)
            piece = slab[ox:ox + blk, oy:oy + cols, oz:oz + depth].reshape(-1, chans)
            total = total + jnp.dot(piece, weights[k], preferred_element_type=jnp.float32)
        return total.reshape(blk, cols, depth, -1)
    starts = (jnp.arange(rows // blk) * blk).astype(jnp.int32)
    return lax.map(one_block, starts).reshape(rows, cols, depth, -1)

def wgrad_whole(field, grad):
    rows, cols, depth, chans = field.shape
    padded = pad_whole(field)
    blk = math.gcd(rows, 16)

    def one_block(start):
        slab = lax.dynamic_slice_in_dim(padded, start, blk + 2, 0)
        gpart = lax.dynamic_slice_in_dim(grad, start, blk, 0).reshape(-1, grad.shape[3])
        terms = []
        for k in range(27):
            ox, oy, oz = (k // 9, k // 3 % 3, k % 3)
            piece = slab[ox:ox + blk, oy:oy + cols, oz:oz + depth].reshape(-1, chans)
            terms.append(jnp.dot(piece.T, gpart, preferred_element_type=jnp.float32))
        return jnp.stack(terms)
    starts = (jnp.arange(rows // blk) * blk).astype(jnp.int32)
    return lax.optimization_barrier(jnp.sum(lax.map(one_block, starts), axis=0))

def flip_taps(weights):
    return jnp.transpose(weights[::-1], (0, 2, 1))

def reference(field_in, w_first, b_first, w_upper, w_second, b_second, cotangent, tile_weights):
    rows, cols = (field_in.shape[0], field_in.shape[1])
    chans = w_first.shape[1]
    depth = field_in.shape[2] // chans
    coarse = field_in.reshape(rows, cols, depth, chans)
    pre_first = conv_whole(coarse, w_first) + b_first
    hidden = act(pre_first).astype(jnp.bfloat16)
    upper_taps = w_upper.astype(jnp.float32).reshape(2, 2, 2, chans, chans)
    upper = jnp.einsum('xyze,abced->xaybzcd', hidden.astype(jnp.float32), upper_taps)
    upper = upper.reshape(2 * rows, 2 * cols, 2 * depth, chans).astype(jnp.bfloat16)
    pre_second = conv_whole(upper, w_second) + b_second
    output_field = act(pre_second).astype(jnp.bfloat16)
    cell_weight = jnp.repeat(jnp.repeat(tile_weights, TT, axis=0), TT, axis=1).astype(jnp.float32)
    fine_cot = cotangent.reshape(2 * rows, 2 * cols, 2 * depth, chans).astype(jnp.float32)
    grad_pre = (cell_weight[:, :, None, None] * fine_cot * slope(pre_second)).astype(jnp.bfloat16)
    grad_upper_field = conv_whole(grad_pre, flip_taps(w_second))
    grad_six = grad_upper_field.reshape(rows, 2, cols, 2, depth, 2, chans)
    grad_hidden = jnp.einsum('xaybzcd,abced->xyze', grad_six, upper_taps)
    grad_pre_first = (grad_hidden * slope(pre_first)).astype(jnp.bfloat16)
    grad_input = conv_whole(grad_pre_first, flip_taps(w_first)).astype(jnp.bfloat16)
    coarse_scale = 1.0 / math.sqrt(rows * cols * depth)
    fine_scale = 1.0 / math.sqrt(8 * rows * cols * depth)
    grad_second = wgrad_whole(upper, grad_pre) * fine_scale
    grad_upper = jnp.einsum('xyze,xaybzcd->abced', hidden.astype(jnp.float32), grad_six)
    grad_upper = grad_upper.reshape(8, chans, chans) * coarse_scale
    grad_first = wgrad_whole(coarse, grad_pre_first) * coarse_scale
    return (output_field.reshape(2 * rows, 2 * cols, 2 * depth * chans), grad_input.reshape(rows, cols, depth * chans), grad_first, grad_upper, grad_second)
```

```python
import functools
import math

import jax
import jax.numpy as jnp
from jax import lax
from jax.experimental import pallas as pl
from jax.experimental.pallas import tpu as pltpu
from jax.sharding import PartitionSpec as P


def extended(cells, sides, width):
    for axis, dim in sides:
        count = lax.axis_size(axis)
        head = lax.slice_in_dim(cells, 0, width, axis=dim)
        tail = lax.slice_in_dim(cells, cells.shape[dim] - width, cells.shape[dim], axis=dim)
        cells = jnp.concatenate(
            [
                lax.ppermute(tail, axis, [(i, (i + 1) % count) for i in range(count)]),
                cells,
                lax.ppermute(head, axis, [((i + 1) % count, i) for i in range(count)]),
            ],
            axis=dim,
        )
    return cells


def act(v):
    return 0.2 * v + 0.8 * jax.nn.softplus(v)


def slope(v):
    return 0.2 + 0.8 * jax.nn.sigmoid(v)


def depth_pad(field):
    return jnp.pad(field, ((0, 0), (0, 0), (1, 1), (0, 0)))


def conv_local(padded, weights, rows, cols):
    depth = padded.shape[2] - 2
    chans = padded.shape[3]
    total = jnp.zeros((rows * cols * depth, weights.shape[2]), jnp.float32)
    for k in range(27):
        ox, oy, oz = (k // 9, k // 3 % 3, k % 3)
        piece = padded[ox : ox + rows, oy : oy + cols, oz : oz + depth].reshape(-1, chans)
        total = total + jnp.dot(piece, weights[k], preferred_element_type=jnp.float32)
    return total.reshape(rows, cols, depth, -1)


def wgrad_local(padded, grad):
    rows, cols, depth, chans = grad.shape
    flat_grad = grad.reshape(-1, chans)
    terms = []
    for k in range(27):
        ox, oy, oz = (k // 9, k // 3 % 3, k % 3)
        piece = padded[ox : ox + rows, oy : oy + cols, oz : oz + depth].reshape(-1, padded.shape[3])
        terms.append(
            lax.dot_general(
                piece, flat_grad, (((0,), (0,)), ((), ())), preferred_element_type=jnp.float32
            )
        )
    return jnp.stack(terms)


def flip_taps(weights):
    return jnp.transpose(weights[::-1], (0, 2, 1))


def upsample(hidden, upper_taps):
    rows, cols, depth, chans = hidden.shape
    fine = jnp.einsum("xyze,abced->xaybzcd", hidden, upper_taps, preferred_element_type=jnp.float32)
    return fine.reshape(2 * rows, 2 * cols, 2 * depth, chans).astype(jnp.bfloat16)


MESH = pl.DeviceIdType.MESH


def add_up(nx, ny, part, full, first_in, line, line_in, sems):
    mx, my = lax.axis_index("gx"), lax.axis_index("gy")
    rows = part.shape[0] // nx
    small = rows // ny
    s1, r1, s2, r2, s3, r3, s4, r4 = sems

    def chunk(i):
        return pl.ds(pl.multiple_of(i * rows, 16), rows)

    def piece(i):
        return pl.ds(pl.multiple_of(i * small, 16), small)

    def along_x(d):
        return lax.rem(mx + d, nx)

    def along_y(d):
        return lax.rem(my + d, ny)

    def spread(copies):
        for copy in copies:
            copy.start()
        return copies

    def finish(copies):
        for copy in copies:
            copy.wait()

    finish(spread([
        pltpu.make_async_remote_copy(
            src_ref=part.at[chunk(along_x(d))], dst_ref=first_in.at[d - 1],
            send_sem=s1.at[d - 1], recv_sem=r1.at[d - 1],
            device_id=(along_x(d), my), device_id_type=MESH)
        for d in range(1, nx)
    ]))
    total = part[chunk(mx), :].astype(jnp.float32)
    for d in range(nx - 1):
        total += first_in[d].astype(jnp.float32)
    line[...] = total.astype(jnp.bfloat16)
    finish(spread([
        pltpu.make_async_remote_copy(
            src_ref=line.at[piece(along_y(d))], dst_ref=line_in.at[d - 1],
            send_sem=s2.at[d - 1], recv_sem=r2.at[d - 1],
            device_id=(mx, along_y(d)), device_id_type=MESH)
        for d in range(1, ny)
    ]))
    total = line[piece(my), :].astype(jnp.float32)
    for d in range(ny - 1):
        total += line_in[d].astype(jnp.float32)
    mine = pl.ds(pl.multiple_of(mx * rows + my * small, 16), small)
    full[mine, :] = total.astype(jnp.bfloat16)
    finish(spread([
        pltpu.make_async_remote_copy(
            src_ref=full.at[mine], dst_ref=full.at[mine],
            send_sem=s3.at[d - 1], recv_sem=r3.at[d - 1],
            device_id=(mx, along_y(d)), device_id_type=MESH)
        for d in range(1, ny)
    ]))
    finish(spread([
        pltpu.make_async_remote_copy(
            src_ref=full.at[chunk(mx)], dst_ref=full.at[chunk(mx)],
            send_sem=s4.at[d - 1], recv_sem=r4.at[d - 1],
            device_id=(along_x(d), my), device_id_type=MESH)
        for d in range(1, nx)
    ]))


def add_up_scratch(nx, ny, height):
    dma = pltpu.SemaphoreType.DMA
    rows = height // nx
    return [
        pltpu.VMEM((nx - 1, rows, 128), jnp.bfloat16),
        pltpu.VMEM((rows, 128), jnp.bfloat16),
        pltpu.VMEM((ny - 1, rows // ny, 128), jnp.bfloat16),
        dma((nx - 1,)), dma((nx - 1,)), dma((ny - 1,)), dma((ny - 1,)),
        dma((ny - 1,)), dma((ny - 1,)), dma((nx - 1,)), dma((nx - 1,)),
    ]


def sum_kernel(nx, ny, part, out, full, first_in, line, line_in, *sems):
    mx, my = lax.axis_index("gx"), lax.axis_index("gy")
    barrier = pltpu.get_barrier_semaphore()
    for d in range(1, nx):
        pl.semaphore_signal(barrier, inc=1, device_id=(lax.rem(mx + d, nx), my), device_id_type=MESH)
    for d in range(1, ny):
        pl.semaphore_signal(barrier, inc=1, device_id=(mx, lax.rem(my + d, ny)), device_id_type=MESH)
    pl.semaphore_wait(barrier, nx + ny - 2)
    add_up(nx, ny, part, full, first_in, line, line_in, sems)
    out[...] = full[...].astype(jnp.float32)


def sum_all(terms):
    nx, ny = lax.axis_size("gx"), lax.axis_size("gy")
    unit = 16 * nx * ny
    flat = jnp.concatenate([t.reshape(-1, 128) for t in terms]).astype(jnp.bfloat16)
    height = -(-flat.shape[0] // unit) * unit
    flat = jnp.pad(flat, ((0, height - flat.shape[0]), (0, 0)))
    total = pl.pallas_call(
        functools.partial(sum_kernel, nx, ny),
        out_shape=jax.ShapeDtypeStruct((height, 128), jnp.float32),
        in_specs=[pl.BlockSpec(memory_space=pltpu.VMEM)],
        out_specs=pl.BlockSpec(memory_space=pltpu.VMEM),
        scratch_shapes=[pltpu.VMEM((height, 128), jnp.bfloat16)] + add_up_scratch(nx, ny, height),
        compiler_params=pltpu.CompilerParams(collective_id=0, has_side_effects=True, vmem_limit_bytes=32 << 20),
    )(flat)
    outs, at = [], 0
    for t in terms:
        size = t.size // 128
        outs.append(total[at : at + size].reshape(t.shape))
        at += size
    return outs


def per_device(field_in, w_first, b_first, w_upper, w_second, b_second, cotangent, tile_weights):
    rows, cols, flat = field_in.shape
    chans = w_first.shape[1]
    depth = flat // chans
    upper_taps = w_upper.reshape(2, 2, 2, chans, chans)
    taps_wide = w_upper.astype(jnp.float32).reshape(2, 2, 2, chans, chans)
    rim = extended(field_in, (("gx", 0), ("gy", 1)), 1)
    input_pad = depth_pad(rim.reshape(rows + 2, cols + 2, depth, chans))
    pre_first = conv_local(input_pad, w_first, rows, cols) + b_first
    hidden = act(pre_first).astype(jnp.bfloat16)
    upper = upsample(hidden, upper_taps)
    upper_cycle = extended(upper.reshape(2 * rows, 2 * cols, 2 * flat), (("gx", 0), ("gy", 1)), 1)
    upper_pad = depth_pad(upper_cycle.reshape(2 * rows + 2, 2 * cols + 2, 2 * depth, chans))
    pre_second = conv_local(upper_pad, w_second, 2 * rows, 2 * cols) + b_second
    output_field = act(pre_second).astype(jnp.bfloat16)
    tiles_x, tiles_y = tile_weights.shape
    side = 2 * rows // tiles_x
    weight_grid = tile_weights.astype(jnp.float32)[:, None, :, None, None, None]
    fine_cot = cotangent.reshape(tiles_x, side, tiles_y, side, 2 * depth, chans).astype(jnp.float32)
    slope_fine = slope(pre_second).reshape(tiles_x, side, tiles_y, side, 2 * depth, chans)
    grad_pre = (
        (weight_grid * fine_cot * slope_fine)
        .reshape(2 * rows, 2 * cols, 2 * depth, chans)
        .astype(jnp.bfloat16)
    )
    devices = lax.axis_size("gx") * lax.axis_size("gy")
    coarse_scale = 1.0 / math.sqrt(rows * cols * depth * devices)
    fine_scale = 1.0 / math.sqrt(8 * rows * cols * depth * devices)
    grad_cycle = extended(grad_pre.reshape(2 * rows, 2 * cols, 2 * flat), (("gx", 0), ("gy", 1)), 1)
    grad_pad = depth_pad(grad_cycle.reshape(2 * rows + 2, 2 * cols + 2, 2 * depth, chans))
    grad_upper_field = conv_local(grad_pad, flip_taps(w_second), 2 * rows, 2 * cols)
    grad_six = grad_upper_field.reshape(rows, 2, cols, 2, depth, 2, chans)
    grad_hidden = jnp.einsum("xaybzcd,abced->xyze", grad_six, taps_wide)
    upper_term = jnp.einsum("xyze,xaybzcd->abced", hidden.astype(jnp.float32), grad_six)
    upper_term = upper_term.reshape(8, chans, chans) * coarse_scale
    grad_pre_first = (grad_hidden * slope(pre_first)).astype(jnp.bfloat16)
    coarse_cycle = extended(grad_pre_first.reshape(rows, cols, flat), (("gx", 0), ("gy", 1)), 1)
    coarse_pad = depth_pad(coarse_cycle.reshape(rows + 2, cols + 2, depth, chans))
    grad_input = conv_local(coarse_pad, flip_taps(w_first), rows, cols).astype(jnp.bfloat16)
    second_term = wgrad_local(upper_pad, grad_pre)
    first_term = wgrad_local(input_pad, grad_pre_first) * coarse_scale
    grad_first, grad_upper, grad_second = sum_all((first_term, upper_term, second_term * fine_scale))
    return (
        output_field.reshape(2 * rows, 2 * cols, 2 * flat),
        grad_input.reshape(rows, cols, flat),
        grad_first,
        grad_upper,
        grad_second,
    )


def solution(mesh):
    in_specs = (P("gx", "gy", None), P(), P(), P(), P(), P(), P("gx", "gy", None), P("gx", "gy"))
    out_specs = (P("gx", "gy", None), P("gx", "gy", None), P(), P(), P())
    return jax.shard_map(
        per_device, mesh=mesh, in_specs=in_specs, out_specs=out_specs, check_vma=False
    )
```

```python
import functools
import math

import jax
import jax.numpy as jnp
from jax import lax
from jax.experimental import pallas as pl
from jax.experimental.pallas import tpu as pltpu
from jax.sharding import PartitionSpec as P


MESH = pl.DeviceIdType.MESH


def add_up(nx, ny, part, full, first_in, line, line_in, sems):
    mx, my = lax.axis_index("gx"), lax.axis_index("gy")
    rows = part.shape[0] // nx
    small = rows // ny
    s1, r1, s2, r2, s3, r3, s4, r4 = sems

    def chunk(i):
        return pl.ds(pl.multiple_of(i * rows, 16), rows)

    def piece(i):
        return pl.ds(pl.multiple_of(i * small, 16), small)

    def along_x(d):
        return lax.rem(mx + d, nx)

    def along_y(d):
        return lax.rem(my + d, ny)

    def spread(copies):
        for copy in copies:
            copy.start()
        return copies

    def finish(copies):
        for copy in copies:
            copy.wait()

    finish(spread([
        pltpu.make_async_remote_copy(
            src_ref=part.at[chunk(along_x(d))], dst_ref=first_in.at[d - 1],
            send_sem=s1.at[d - 1], recv_sem=r1.at[d - 1],
            device_id=(along_x(d), my), device_id_type=MESH)
        for d in range(1, nx)
    ]))
    total = part[chunk(mx), :].astype(jnp.float32)
    for d in range(nx - 1):
        total += first_in[d].astype(jnp.float32)
    line[...] = total.astype(jnp.bfloat16)
    finish(spread([
        pltpu.make_async_remote_copy(
            src_ref=line.at[piece(along_y(d))], dst_ref=line_in.at[d - 1],
            send_sem=s2.at[d - 1], recv_sem=r2.at[d - 1],
            device_id=(mx, along_y(d)), device_id_type=MESH)
        for d in range(1, ny)
    ]))
    total = line[piece(my), :].astype(jnp.float32)
    for d in range(ny - 1):
        total += line_in[d].astype(jnp.float32)
    mine = pl.ds(pl.multiple_of(mx * rows + my * small, 16), small)
    full[mine, :] = total.astype(jnp.bfloat16)
    finish(spread([
        pltpu.make_async_remote_copy(
            src_ref=full.at[mine], dst_ref=full.at[mine],
            send_sem=s3.at[d - 1], recv_sem=r3.at[d - 1],
            device_id=(mx, along_y(d)), device_id_type=MESH)
        for d in range(1, ny)
    ]))
    finish(spread([
        pltpu.make_async_remote_copy(
            src_ref=full.at[chunk(mx)], dst_ref=full.at[chunk(mx)],
            send_sem=s4.at[d - 1], recv_sem=r4.at[d - 1],
            device_id=(along_x(d), my), device_id_type=MESH)
        for d in range(1, nx)
    ]))


def add_up_scratch(nx, ny, height):
    dma = pltpu.SemaphoreType.DMA
    rows = height // nx
    return [
        pltpu.VMEM((nx - 1, rows, 128), jnp.bfloat16),
        pltpu.VMEM((rows, 128), jnp.bfloat16),
        pltpu.VMEM((ny - 1, rows // ny, 128), jnp.bfloat16),
        dma((nx - 1,)), dma((nx - 1,)), dma((ny - 1,)), dma((ny - 1,)),
        dma((ny - 1,)), dma((ny - 1,)), dma((nx - 1,)), dma((nx - 1,)),
    ]


AROUND = [(dx, dy) for dx in (-1, 0, 1) for dy in (-1, 0, 1) if (dx, dy) != (0, 0)]


def act(v, small):
    return 0.2 * v + 0.8 * (jnp.maximum(v, 0.0) + jnp.log(1.0 + small))


def slope(v, small):
    share = 1.0 / (1.0 + small)
    return 0.2 + 0.8 * jnp.where(v >= 0.0, share, small * share)


def leaving(step, size, width):
    return {1: pl.ds(size - width, width), -1: pl.ds(0, width), 0: pl.ds(0, size)}[step]


def landing(step, size, width):
    return {1: pl.ds(0, width), -1: pl.ds(width + size, width), 0: pl.ds(width, size)}[step]


def rim_copies(nx, ny, src, dst, width, send, recv, whole=False):
    mx, my = lax.axis_index("gx"), lax.axis_index("gy")
    copies = []
    for k, (dx, dy) in enumerate(AROUND):
        if whole:
            part, spot = src, dst.at[1 - dx, 1 - dy]
        else:
            part = src.at[leaving(dx, src.shape[0], width), leaving(dy, src.shape[1], width)]
            spot = dst.at[landing(dx, src.shape[0], width), landing(dy, src.shape[1], width)]
        copies.append(pltpu.make_async_remote_copy(
            src_ref=part, dst_ref=spot, send_sem=send.at[k], recv_sem=recv.at[k],
            device_id=(lax.rem(mx + dx + nx, nx), lax.rem(my + dy + ny, ny)), device_id_type=MESH))
    return copies


def shifted(cells):
    flat = cells.reshape((-1,) + cells.shape[-2:])
    depth = flat.shape[1]
    place = lax.broadcasted_iota(jnp.int32, flat.shape, 1)
    lower = jnp.where(place == 0, 0.0, pltpu.roll(flat, 1, 1))
    upper = jnp.where(place == depth - 1, 0.0, pltpu.roll(flat, depth - 1, 1))
    return lower.reshape(cells.shape), upper.reshape(cells.shape)


def coarse_taps(cells):
    cells = cells.astype(jnp.float32)
    lower, upper = shifted(cells)
    return jnp.concatenate([lower, cells, upper], axis=-1).astype(jnp.bfloat16)


def fine_taps(cells):
    lower, upper = shifted(cells)
    lane = lax.broadcasted_iota(jnp.int32, cells.shape, cells.ndim - 1)
    return jnp.where(lane < cells.shape[-1] // 2, upper, lower).astype(jnp.bfloat16)


def conv(taps, weights, start, rows, cols):
    total = None
    for k in range(9):
        ox, oy = start + k // 3, start + k % 3
        piece = taps[ox : ox + rows, oy : oy + cols]
        piece = piece.reshape(-1, piece.shape[-1])
        term = jnp.dot(piece, weights[k], preferred_element_type=jnp.float32)
        total = term if total is None else total + term
    return total.reshape(rows, cols, -1, weights.shape[2])


def spread_edge(values, axis, inner):
    first, mid, last = values
    shape = list(mid.shape)
    shape[axis] = inner
    return jnp.concatenate([first, jnp.broadcast_to(mid, shape), last], axis=axis)


def block_kernel(nx, ny, fine_scale, coarse_scale, field, cot, tile, w_first, w_first_t, b_first, w_upper, w_upper_t,
                 w_second, w_second_t, b_second, out_field, out_grad, out_sums,
                 field_ext, cot_ext, tile_ext, ctaps, ftaps, gtaps, rim_ext, rim_out, part, full,
                 first_in, line, line_in, s_f, r_f, s_c, r_c, s_t, r_t, s_g, r_g, *sems):
    mx, my = lax.axis_index("gx"), lax.axis_index("gy")
    rows, cols, depth, chans = field.shape
    fr, fc = 2 * rows, 2 * cols
    barrier = pltpu.get_barrier_semaphore()
    peers = {((dx + nx) % nx, (dy + ny) % ny) for dx, dy in AROUND}
    peers |= {(d, 0) for d in range(1, nx)} | {(0, d) for d in range(1, ny)}
    for dx, dy in sorted(peers):
        pl.semaphore_signal(barrier, inc=1, device_id=(lax.rem(mx + dx, nx), lax.rem(my + dy, ny)), device_id_type=MESH)
    pl.semaphore_wait(barrier, len(peers))
    field_copies = rim_copies(nx, ny, field, field_ext, 2, s_f, r_f)
    cot_copies = rim_copies(nx, ny, cot, cot_ext, 1, s_c, r_c)
    tile_copies = rim_copies(nx, ny, tile, tile_ext, 1, s_t, r_t, True)
    for copy in field_copies + cot_copies + tile_copies:
        copy.start()
    field_ext[2 : 2 + rows, 2 : 2 + cols] = field[...]
    cot_ext[1 : 1 + fr, 1 : 1 + fc] = cot[...]
    tile_ext[1, 1] = tile[...]
    for copy in field_copies:
        copy.wait()

    ctaps[...] = coarse_taps(field_ext[...])
    pre_first = conv(ctaps, w_first, 0, rows + 2, cols + 2) + b_first[...]
    small = jnp.exp(-jnp.abs(pre_first))
    hidden = act(pre_first, small).astype(jnp.bfloat16)
    slope_first = slope(pre_first, small)[1 : 1 + rows, 1 : 1 + cols]
    upper = jnp.dot(hidden.reshape(-1, chans), w_upper[...], preferred_element_type=jnp.float32)
    upper = upper.reshape(rows + 2, cols + 2, depth, 8 * chans)
    wide = 2 * chans
    sides = []
    for a in (0, 1):
        pair = [upper[..., (2 * a + b) * wide : (2 * a + b + 1) * wide] for b in (0, 1)]
        sides.append(jnp.stack(pair, axis=2).reshape(rows + 2, fc + 4, depth, wide))
    upper = jnp.stack(sides, axis=1).reshape(fr + 4, fc + 4, depth, wide)
    ftaps[..., :wide] = upper.astype(jnp.bfloat16)
    ftaps[..., wide:] = fine_taps(ftaps[..., :wide].astype(jnp.float32))

    pre_second = conv(ftaps, w_second, 0, fr + 2, fc + 2) + b_second[...]
    small = jnp.exp(-jnp.abs(pre_second))
    out_field[...] = act(pre_second, small)[1 : 1 + fr, 1 : 1 + fc].astype(jnp.bfloat16)
    for copy in cot_copies + tile_copies:
        copy.wait()
    tiles = tile_ext[...].astype(jnp.float32)
    bands = [spread_edge([tiles[i, j][None] for j in range(3)], 0, fc)[None] for i in range(3)]
    weight = spread_edge(bands, 0, fr)
    grad_pre = weight * cot_ext[...].astype(jnp.float32) * slope(pre_second, small)
    gtaps[..., :wide] = grad_pre.astype(jnp.bfloat16)
    gtaps[..., wide:] = fine_taps(gtaps[..., :wide].astype(jnp.float32))

    grad_up = conv(gtaps, w_second_t, 0, fr, fc).astype(jnp.bfloat16)
    six = grad_up.reshape(rows, 2, cols, 2, depth, wide)
    corner = {(a, b): six[:, a, :, b].reshape(-1, wide) for a in (0, 1) for b in (0, 1)}
    grad_hidden = sum(
        jnp.dot(corner[a, b], w_upper_t[2 * a + b], preferred_element_type=jnp.float32)
        for a in (0, 1) for b in (0, 1)
    )
    grad_first = (grad_hidden.reshape(rows, cols, depth, chans) * slope_first).astype(jnp.bfloat16)
    rim_out[...] = grad_first
    rim_ext[1 : 1 + rows, 1 : 1 + cols] = grad_first
    rim = rim_copies(nx, ny, rim_out, rim_ext, 1, s_g, r_g)
    for copy in rim:
        copy.start()

    part[31 * chans :, :] = jnp.zeros((part.shape[0] - 31 * chans, 128), jnp.bfloat16)
    own_hidden = hidden[1 : 1 + rows, 1 : 1 + cols].reshape(-1, chans)
    hidden_t = own_hidden.astype(jnp.float32).T.astype(jnp.bfloat16)
    for a in (0, 1):
        for b in (0, 1):
            at = (27 + 2 * a + b) * chans
            term = jnp.dot(hidden_t, corner[a, b], preferred_element_type=jnp.float32)
            part[at : at + chans, :] = (term * coarse_scale).astype(jnp.bfloat16)
    own_grad = gtaps[1 : 1 + fr, 1 : 1 + fc, :, :wide].reshape(-1, wide)
    own_grad_t = own_grad.astype(jnp.float32).T.astype(jnp.bfloat16)
    first_t = grad_first.reshape(-1, chans).astype(jnp.float32).T.astype(jnp.bfloat16)
    for k in range(9):
        ox, oy = k // 3, k % 3
        piece = ftaps[1 + ox : 1 + ox + fr, 1 + oy : 1 + oy + fc].reshape(-1, 2 * wide)
        two = jnp.dot(own_grad_t, piece, preferred_element_type=jnp.float32) * fine_scale
        even, odd = two[:chans], two[chans:]
        tap0 = odd[:, :chans] + even[:, 3 * chans :]
        tap1 = even[:, :chans] + odd[:, chans : 2 * chans]
        tap2 = even[:, chans : 2 * chans] + odd[:, 2 * chans : 3 * chans]
        piece = ctaps[1 + ox : 1 + ox + rows, 1 + oy : 1 + oy + cols].reshape(-1, 3 * chans)
        one = jnp.dot(first_t, piece, preferred_element_type=jnp.float32) * coarse_scale
        at = 3 * k * chans
        part[at : at + chans, :] = jnp.concatenate([tap0, tap1], axis=1).astype(jnp.bfloat16)
        part[at + chans : at + 2 * chans, :] = one[:, :wide].astype(jnp.bfloat16)
        part[at + 2 * chans : at + 3 * chans, :] = jnp.concatenate([tap2, one[:, wide:]], axis=1).astype(jnp.bfloat16)

    for copy in rim:
        copy.wait()
    grad_in = conv(coarse_taps(rim_ext[...]), w_first_t, 0, rows, cols)
    out_grad[...] = grad_in.astype(jnp.bfloat16)
    add_up(nx, ny, part, full, first_in, line, line_in, sems)
    out_sums[...] = full[...].astype(jnp.float32)


def flip_taps(weights):
    return jnp.transpose(weights[::-1], (0, 2, 1))


def pair_taps(weights):
    w = weights.reshape(9, 3, weights.shape[1], weights.shape[2])
    none = jnp.zeros_like(w[:, 0])
    even = jnp.concatenate([w[:, 1], w[:, 2], none, w[:, 0]], axis=1)
    odd = jnp.concatenate([w[:, 0], w[:, 1], w[:, 2], none], axis=1)
    return jnp.concatenate([even, odd], axis=2)


def per_device(field_in, w_first, b_first, w_upper, w_second, b_second, cotangent, tile_weights):
    rows, cols, flat = field_in.shape
    chans = w_first.shape[1]
    depth = flat // chans
    wide = 2 * chans
    nx, ny = lax.axis_size("gx"), lax.axis_size("gy")
    coarse_scale = 1.0 / math.sqrt(rows * cols * depth * nx * ny)
    fine_scale = 1.0 / math.sqrt(8 * rows * cols * depth * nx * ny)
    fr, fc = 2 * rows, 2 * cols
    unit = 16 * nx * ny
    height = -(-31 * chans // unit) * unit
    bf, dma = jnp.bfloat16, pltpu.SemaphoreType.DMA
    tile = jnp.broadcast_to(tile_weights.astype(bf), (16, wide))
    up = w_upper.reshape(4, 2, chans, chans)
    args = (
        field_in.reshape(rows, cols, depth, chans),
        cotangent.reshape(fr, fc, depth, wide),
        tile,
        w_first.reshape(9, 3 * chans, chans),
        flip_taps(w_first).reshape(9, 3 * chans, chans),
        b_first.reshape(1, chans),
        jnp.transpose(w_upper, (1, 0, 2)).reshape(chans, 8 * chans),
        jnp.transpose(up, (0, 1, 3, 2)).reshape(4, wide, chans),
        pair_taps(w_second),
        pair_taps(flip_taps(w_second)),
        jnp.concatenate([b_second, b_second]).reshape(1, wide),
    )
    vmem = pl.BlockSpec(memory_space=pltpu.VMEM)
    out, grad, sums = pl.pallas_call(
        functools.partial(block_kernel, nx, ny, fine_scale, coarse_scale),
        out_shape=(
            jax.ShapeDtypeStruct((fr, fc, depth, wide), bf),
            jax.ShapeDtypeStruct((rows, cols, depth, chans), bf),
            jax.ShapeDtypeStruct((height, 128), jnp.float32),
        ),
        in_specs=[vmem] * len(args),
        out_specs=(vmem, vmem, vmem),
        scratch_shapes=[
            pltpu.VMEM((rows + 4, cols + 4, depth, chans), bf),
            pltpu.VMEM((fr + 2, fc + 2, depth, wide), bf),
            pltpu.VMEM((3, 3, 16, wide), bf),
            pltpu.VMEM((rows + 4, cols + 4, depth, 3 * chans), bf),
            pltpu.VMEM((fr + 4, fc + 4, depth, 2 * wide), bf),
            pltpu.VMEM((fr + 2, fc + 2, depth, 2 * wide), bf),
            pltpu.VMEM((rows + 2, cols + 2, depth, chans), bf),
            pltpu.VMEM((rows, cols, depth, chans), bf),
            pltpu.VMEM((height, 128), bf),
            pltpu.VMEM((height, 128), bf),
        ] + add_up_scratch(nx, ny, height)[:3] + [dma((8,))] * 8 + add_up_scratch(nx, ny, height)[3:],
        compiler_params=pltpu.CompilerParams(collective_id=0, has_side_effects=True, vmem_limit_bytes=48 << 20),
    )(*args)
    taps = sums[: 27 * chans].reshape(9, 3, chans, 2, chans)
    second = jnp.stack([taps[:, 0, :, 0], taps[:, 0, :, 1], taps[:, 2, :, 0]], axis=1)
    first = jnp.stack([taps[:, 1, :, 0], taps[:, 1, :, 1], taps[:, 2, :, 1]], axis=1)
    upper = sums[27 * chans : 31 * chans].reshape(4, chans, 2, chans)
    return (
        out.reshape(fr, fc, 2 * flat),
        grad.reshape(rows, cols, flat),
        jnp.transpose(first.reshape(27, chans, chans), (0, 2, 1)),
        jnp.transpose(upper, (0, 2, 1, 3)).reshape(8, chans, chans),
        jnp.transpose(second.reshape(27, chans, chans), (0, 2, 1)),
    )


def solution(mesh):
    in_specs = (P("gx", "gy", None), P(), P(), P(), P(), P(), P("gx", "gy", None), P("gx", "gy"))
    out_specs = (P("gx", "gy", None), P("gx", "gy", None), P(), P(), P())
    return jax.shard_map(
        per_device, mesh=mesh, in_specs=in_specs, out_specs=out_specs, check_vma=False
    )
```

```python
import functools
import math

import jax
import jax.numpy as jnp
from jax import lax
from jax.experimental import pallas as pl
from jax.experimental.pallas import tpu as pltpu
from jax.sharding import PartitionSpec as P


MESH = pl.DeviceIdType.MESH


def add_up(nx, ny, used, part, full, first_in, line, line_in, sems):
    mx, my = lax.axis_index("gx"), lax.axis_index("gy")
    small = part.shape[1] // ny
    s1, r1, s2, r2, s3, r3, s4, r4 = sems

    def piece(i):
        return pl.ds(pl.multiple_of(i * small, 16), small)

    def along_x(d):
        return lax.rem(mx + d, nx)

    def along_y(d):
        return lax.rem(my + d, ny)

    def over_x(pair, send, recv):
        copies = [
            pltpu.make_async_remote_copy(
                src_ref=pair(d)[0], dst_ref=pair(d)[1], send_sem=send.at[d - 1], recv_sem=recv.at[d - 1],
                device_id=(along_x(d), my), device_id_type=MESH)
            for d in range(1, nx)
        ]
        for copy in copies:
            copy.start()
        return copies

    def over_y(pair, send, recv):
        copies = [
            pltpu.make_async_remote_copy(
                src_ref=pair(d)[0], dst_ref=pair(d)[1], send_sem=send.at[d - 1], recv_sem=recv.at[d - 1],
                device_id=(mx, along_y(d)), device_id_type=MESH)
            for d in range(1, ny)
        ]
        for copy in copies:
            copy.start()
        return copies

    copies = over_x(lambda d: (part.at[along_x(d), pl.ds(0, used)], first_in.at[d - 1]), s1, r1)
    yield
    for copy in copies:
        copy.wait()
    total = part[mx, :used, :].astype(jnp.float32)
    for d in range(nx - 1):
        total += first_in[d].astype(jnp.float32)
    line[:used, :] = total.astype(jnp.bfloat16)
    if used < line.shape[0]:
        line[used:, :] = jnp.zeros((line.shape[0] - used, 128), jnp.bfloat16)
    copies = over_y(lambda d: (line.at[piece(along_y(d))], line_in.at[d - 1]), s2, r2)
    yield
    for copy in copies:
        copy.wait()
    total = line[piece(my), :].astype(jnp.float32)
    for d in range(ny - 1):
        total += line_in[d].astype(jnp.float32)
    full[mx, piece(my), :] = total.astype(jnp.bfloat16)
    copies = over_y(lambda d: (full.at[mx, piece(my)], full.at[mx, piece(my)]), s3, r3)
    yield
    for copy in copies:
        copy.wait()
    whole = pl.ds(0, used)
    copies = over_x(lambda d: (full.at[mx, whole], full.at[mx, whole]), s4, r4)
    yield
    for copy in copies:
        copy.wait()


def sum_sizes(nx, ny, blocks, chans):
    used = -(-blocks * chans // (16 * nx)) * 16
    return used, -(-used // (16 * ny)) * 16 * ny


def add_up_scratch(nx, ny, blocks, chans):
    used, chunk = sum_sizes(nx, ny, blocks, chans)
    bf, dma = jnp.bfloat16, pltpu.SemaphoreType.DMA
    return [
        pltpu.VMEM((nx, chunk, 128), bf),
        pltpu.VMEM((nx, chunk, 128), bf),
        pltpu.VMEM((nx - 1, used, 128), bf),
        pltpu.VMEM((chunk, 128), bf),
        pltpu.VMEM((ny - 1, chunk // ny, 128), bf),
        dma((nx - 1,)), dma((nx - 1,)), dma((ny - 1,)), dma((ny - 1,)),
        dma((ny - 1,)), dma((ny - 1,)), dma((nx - 1,)), dma((nx - 1,)),
    ]


def segments(used, start, stop):
    found = []
    while start < stop:
        chunk, row = start // used, start % used
        size = min(used - row, stop - start)
        found.append((chunk, row, size))
        start += size
    return found


def put_block(part, used, block, value):
    at, value = 0, value.astype(jnp.bfloat16)
    height = value.shape[0]
    for chunk, row, size in segments(used, block * height, (block + 1) * height):
        part[chunk, row : row + size, :] = value[at : at + size]
        at += size


def put_taps(part, used, terms):
    wide = part.shape[2]
    for k in range(9):
        put_block(part, used, k, terms[k][:, :wide])
    for j in range(5):
        left = terms[2 * j][:, wide:]
        right = terms[2 * j + 1][:, wide:] if 2 * j + 1 < 9 else jnp.zeros_like(left)
        put_block(part, used, 9 + j, jnp.concatenate([left, right], axis=1))


def clear_end(part, used, rows):
    for chunk, row, size in segments(used, rows, part.shape[0] * used):
        part[chunk, row : row + size, :] = jnp.zeros((size, part.shape[2]), jnp.bfloat16)


def get_block(full, used, block, height):
    pieces = [full[c, r : r + n, :] for c, r, n in segments(used, block * height, (block + 1) * height)]
    return jnp.concatenate(pieces, axis=0).astype(jnp.float32) if len(pieces) > 1 else pieces[0].astype(jnp.float32)


def get_taps(full, used, out):
    chans = out.shape[1]
    for k in range(9):
        out[3 * k : 3 * k + 2] = get_block(full, used, k, chans).T.reshape(2, chans, chans)
    for j in range(5):
        both = get_block(full, used, 9 + j, chans).T
        out[6 * j + 2] = both[:chans]
        if 2 * j + 1 < 9:
            out[6 * j + 5] = both[chans:]


AROUND = [(dx, dy) for dx in (-1, 0, 1) for dy in (-1, 0, 1) if (dx, dy) != (0, 0)]


def act(v, small):
    return 0.2 * v + 0.8 * (jnp.maximum(v, 0.0) + jnp.log(1.0 + small))


def slope(v, small):
    share = 1.0 / (1.0 + small)
    return 0.2 + 0.8 * jnp.where(v >= 0.0, share, small * share)


def leaving(step, size, width):
    return {1: pl.ds(size - width, width), -1: pl.ds(0, width), 0: pl.ds(0, size)}[step]


def landing(step, size, width):
    return {1: pl.ds(0, width), -1: pl.ds(width + size, width), 0: pl.ds(width, size)}[step]


def rim_copies(nx, ny, src, dst, width, send, recv, whole=False):
    mx, my = lax.axis_index("gx"), lax.axis_index("gy")
    copies = []
    for k, (dx, dy) in enumerate(AROUND):
        if whole:
            part, spot = src, dst.at[1 - dx, 1 - dy]
        else:
            part = src.at[leaving(dx, src.shape[0], width), leaving(dy, src.shape[1], width)]
            spot = dst.at[landing(dx, src.shape[0], width), landing(dy, src.shape[1], width)]
        copies.append(pltpu.make_async_remote_copy(
            src_ref=part, dst_ref=spot, send_sem=send.at[k], recv_sem=recv.at[k],
            device_id=(lax.rem(mx + dx + nx, nx), lax.rem(my + dy + ny, ny)), device_id_type=MESH))
    return copies


def shifted(cells):
    flat = cells.reshape((-1,) + cells.shape[-2:])
    depth = flat.shape[1]
    place = lax.broadcasted_iota(jnp.int32, flat.shape, 1)
    lower = jnp.where(place == 0, 0.0, pltpu.roll(flat, 1, 1))
    upper = jnp.where(place == depth - 1, 0.0, pltpu.roll(flat, depth - 1, 1))
    return lower.reshape(cells.shape), upper.reshape(cells.shape)


def coarse_taps(cells):
    cells = cells.astype(jnp.float32)
    lower, upper = shifted(cells)
    return jnp.concatenate([lower, cells, upper], axis=-1).astype(jnp.bfloat16)


def fine_taps(cells):
    lower, upper = shifted(cells)
    lane = lax.broadcasted_iota(jnp.int32, cells.shape, cells.ndim - 1)
    return jnp.where(lane < cells.shape[-1] // 2, upper, lower).astype(jnp.bfloat16)


def times(left, right):
    return jnp.dot(left, right, preferred_element_type=jnp.float32)


def times_t(left, right):
    return lax.dot_general(left, right, (((1,), (1,)), ((), ())), preferred_element_type=jnp.float32)


def conv(taps, weights, rows, cols, product=times):
    total = None
    for k in range(9):
        ox, oy = k // 3, k % 3
        piece = taps[ox : ox + rows, oy : oy + cols]
        piece = piece.reshape(-1, piece.shape[-1])
        term = product(piece, weights[k])
        total = term if total is None else total + term
    return total.reshape(rows, cols, -1, total.shape[1])


def spread_edge(values, axis, inner):
    first, mid, last = values
    shape = list(mid.shape)
    shape[axis] = inner
    return jnp.concatenate([first, jnp.broadcast_to(mid, shape), last], axis=axis)


def block_kernel(nx, ny, fine_scale, coarse_scale, field, cot, tile, w_first, b_first, w_upper, w_second, b_second,
                 out_field, out_grad, out_first, out_upper, out_second,
                 field_ext, cot_ext, tile_ext, ctaps, ftaps, gtaps, rim_ext, rim_out,
                 first_t, up_row, second_n, second_t, s_f, r_f, s_c, r_c, s_t, r_t, s_g, r_g, *groups):
    mx, my = lax.axis_index("gx"), lax.axis_index("gy")
    rows, cols, depth, chans = field.shape
    fr, fc = 2 * rows, 2 * cols
    wide = 2 * chans
    part_a, full_a, *rest_a = groups[: len(groups) // 2]
    part_b, full_b, *rest_b = groups[len(groups) // 2 :]
    used_a, used_b = rest_a[0].shape[1], rest_b[0].shape[1]
    barrier = pltpu.get_barrier_semaphore()
    peers = {((dx + nx) % nx, (dy + ny) % ny) for dx, dy in AROUND}
    peers |= {(d, 0) for d in range(1, nx)} | {(0, d) for d in range(1, ny)}
    for dx, dy in sorted(peers):
        pl.semaphore_signal(barrier, inc=1, device_id=(lax.rem(mx + dx, nx), lax.rem(my + dy, ny)), device_id_type=MESH)
    pl.semaphore_wait(barrier, len(peers))
    field_copies = rim_copies(nx, ny, field, field_ext, 2, s_f, r_f)
    cot_copies = rim_copies(nx, ny, cot, cot_ext, 1, s_c, r_c)
    tile_copies = rim_copies(nx, ny, tile, tile_ext, 1, s_t, r_t, True)
    for copy in field_copies + cot_copies + tile_copies:
        copy.start()
    field_ext[2 : 2 + rows, 2 : 2 + cols] = field[...]
    cot_ext[1 : 1 + fr, 1 : 1 + fc] = cot[...]
    tile_ext[1, 1] = tile[...]
    none = jnp.zeros((chans, chans), jnp.bfloat16)
    for k in range(9):
        low, mid, high = w_second[3 * k], w_second[3 * k + 1], w_second[3 * k + 2]
        second_n[k, :chans] = jnp.concatenate([mid, low], axis=1)
        second_n[k, chans : 2 * chans] = jnp.concatenate([high, mid], axis=1)
        second_n[k, 2 * chans : 3 * chans] = jnp.concatenate([none, high], axis=1)
        second_n[k, 3 * chans :] = jnp.concatenate([low, none], axis=1)
        second_t[8 - k, :chans] = jnp.concatenate([mid, low, none, high], axis=1)
        second_t[8 - k, chans:] = jnp.concatenate([high, mid, low, none], axis=1)
        first_t[8 - k] = jnp.concatenate([w_first[3 * k + 2], w_first[3 * k + 1], w_first[3 * k]], axis=1)
    up_row[...] = jnp.concatenate([w_upper[k] for k in range(8)], axis=1)
    for copy in field_copies:
        copy.wait()

    ctaps[...] = coarse_taps(field_ext[...])
    pre_first = conv(ctaps, w_first[...].reshape(9, 3 * chans, chans), rows + 2, cols + 2) + b_first[...]
    small = jnp.exp(-jnp.abs(pre_first))
    hidden = act(pre_first, small).astype(jnp.bfloat16)
    slope_first = slope(pre_first, small)[1 : 1 + rows, 1 : 1 + cols]
    upper = times(hidden.reshape(-1, chans), up_row[...])
    upper = upper.reshape(rows + 2, cols + 2, depth, 8 * chans)
    sides = []
    for a in (0, 1):
        pair = [upper[..., (2 * a + b) * wide : (2 * a + b + 1) * wide] for b in (0, 1)]
        sides.append(jnp.stack(pair, axis=2).reshape(rows + 2, fc + 4, depth, wide))
    upper = jnp.stack(sides, axis=1).reshape(fr + 4, fc + 4, depth, wide)
    ftaps[..., :wide] = upper.astype(jnp.bfloat16)
    ftaps[..., wide:] = fine_taps(ftaps[..., :wide].astype(jnp.float32))

    pre_second = conv(ftaps, second_n, fr + 2, fc + 2) + b_second[...]
    small = jnp.exp(-jnp.abs(pre_second))
    out_field[...] = act(pre_second, small)[1 : 1 + fr, 1 : 1 + fc].astype(jnp.bfloat16)
    for copy in cot_copies + tile_copies:
        copy.wait()
    tiles = tile_ext[...].astype(jnp.float32)
    bands = [spread_edge([tiles[i, j][None] for j in range(3)], 0, fc)[None] for i in range(3)]
    weight = spread_edge(bands, 0, fr)
    grad_pre = weight * cot_ext[...].astype(jnp.float32) * slope(pre_second, small)
    gtaps[..., :wide] = grad_pre.astype(jnp.bfloat16)
    gtaps[..., wide:] = fine_taps(gtaps[..., :wide].astype(jnp.float32))

    own_grad = gtaps[1 : 1 + fr, 1 : 1 + fc, :, :wide].reshape(-1, wide)
    own_grad_t = own_grad.astype(jnp.float32).T.astype(jnp.bfloat16)
    terms = []
    for k in range(9):
        ox, oy = 1 + k // 3, 1 + k % 3
        piece = ftaps[ox : ox + fr, oy : oy + fc].reshape(-1, 2 * wide)
        two = times(own_grad_t, piece) * fine_scale
        even, odd = two[:chans], two[chans:]
        tap0 = odd[:, :chans] + even[:, 3 * chans :]
        tap1 = even[:, :chans] + odd[:, chans : 2 * chans]
        tap2 = even[:, chans : 2 * chans] + odd[:, 2 * chans : 3 * chans]
        terms.append(jnp.concatenate([tap0, tap1, tap2], axis=1))
    put_taps(part_a, used_a, terms)
    clear_end(part_a, used_a, 14 * chans)
    sum_a = add_up(nx, ny, used_a, part_a, full_a, *rest_a[:3], rest_a[3:])
    next(sum_a)

    grad_up = conv(gtaps, second_t, fr, fc, times_t).astype(jnp.bfloat16)
    six = grad_up.reshape(rows, 2, cols, 2, depth, wide)
    corner = [six[:, a, :, b].reshape(-1, wide) for a in (0, 1) for b in (0, 1)]
    grad_hidden = times_t(jnp.concatenate(corner, axis=1), up_row[...])
    grad_first = (grad_hidden.reshape(rows, cols, depth, chans) * slope_first).astype(jnp.bfloat16)
    rim_out[...] = grad_first
    rim_ext[1 : 1 + rows, 1 : 1 + cols] = grad_first
    rim = rim_copies(nx, ny, rim_out, rim_ext, 1, s_g, r_g)
    for copy in rim:
        copy.start()
    next(sum_a)

    own_hidden = hidden[1 : 1 + rows, 1 : 1 + cols].reshape(-1, chans)
    hidden_t = own_hidden.astype(jnp.float32).T.astype(jnp.bfloat16)
    for k in range(4):
        put_block(part_b, used_b, 14 + k, times(hidden_t, corner[k]) * coarse_scale)
    grad_first_t = grad_first.reshape(-1, chans).astype(jnp.float32).T.astype(jnp.bfloat16)
    terms = []
    for k in range(9):
        ox, oy = 1 + k // 3, 1 + k % 3
        piece = ctaps[ox : ox + rows, oy : oy + cols].reshape(-1, 3 * chans)
        terms.append(times(grad_first_t, piece) * coarse_scale)
    put_taps(part_b, used_b, terms)
    clear_end(part_b, used_b, 18 * chans)
    sum_b = add_up(nx, ny, used_b, part_b, full_b, *rest_b[:3], rest_b[3:])
    next(sum_b)
    next(sum_a)
    for copy in rim:
        copy.wait()
    grad_in = conv(coarse_taps(rim_ext[...]), first_t, rows, cols, times_t)
    out_grad[...] = grad_in.astype(jnp.bfloat16)
    next(sum_a)
    next(sum_b)
    next(sum_b)
    next(sum_b)
    for _ in sum_a:
        pass
    get_taps(full_a, used_a, out_second)
    for _ in sum_b:
        pass
    get_taps(full_b, used_b, out_first)
    for k in range(4):
        both = get_block(full_b, used_b, 14 + k, chans)
        out_upper[2 * k] = both[:, :chans]
        out_upper[2 * k + 1] = both[:, chans:]


def per_device(field_in, w_first, b_first, w_upper, w_second, b_second, cotangent, tile_weights):
    rows, cols, flat = field_in.shape
    chans = w_first.shape[1]
    depth = flat // chans
    wide = 2 * chans
    nx, ny = lax.axis_size("gx"), lax.axis_size("gy")
    coarse_scale = 1.0 / math.sqrt(rows * cols * depth * nx * ny)
    fine_scale = 1.0 / math.sqrt(8 * rows * cols * depth * nx * ny)
    fr, fc = 2 * rows, 2 * cols
    bf, dma = jnp.bfloat16, pltpu.SemaphoreType.DMA
    args = (
        field_in.reshape(rows, cols, depth, chans),
        cotangent.reshape(fr, fc, depth, wide),
        jnp.broadcast_to(tile_weights.astype(bf), (16, wide)),
        w_first,
        b_first.reshape(1, chans),
        w_upper,
        w_second,
        jnp.concatenate([b_second, b_second]).reshape(1, wide),
    )
    vmem = pl.BlockSpec(memory_space=pltpu.VMEM)
    out, grad, first, upper, second = pl.pallas_call(
        functools.partial(block_kernel, nx, ny, fine_scale, coarse_scale),
        out_shape=(
            jax.ShapeDtypeStruct((fr, fc, depth, wide), bf),
            jax.ShapeDtypeStruct((rows, cols, depth, chans), bf),
            jax.ShapeDtypeStruct((27, chans, chans), jnp.float32),
            jax.ShapeDtypeStruct((8, chans, chans), jnp.float32),
            jax.ShapeDtypeStruct((27, chans, chans), jnp.float32),
        ),
        in_specs=[vmem] * len(args),
        out_specs=(vmem,) * 5,
        scratch_shapes=[
            pltpu.VMEM((rows + 4, cols + 4, depth, chans), bf),
            pltpu.VMEM((fr + 2, fc + 2, depth, wide), bf),
            pltpu.VMEM((3, 3, 16, wide), bf),
            pltpu.VMEM((rows + 4, cols + 4, depth, 3 * chans), bf),
            pltpu.VMEM((fr + 4, fc + 4, depth, 2 * wide), bf),
            pltpu.VMEM((fr + 2, fc + 2, depth, 2 * wide), bf),
            pltpu.VMEM((rows + 2, cols + 2, depth, chans), bf),
            pltpu.VMEM((rows, cols, depth, chans), bf),
            pltpu.VMEM((9, chans, 3 * chans), bf),
            pltpu.VMEM((chans, 8 * chans), bf),
            pltpu.VMEM((9, 2 * wide, wide), bf),
            pltpu.VMEM((9, wide, 2 * wide), bf),
        ] + [dma((8,))] * 8 + add_up_scratch(nx, ny, 14, chans) + add_up_scratch(nx, ny, 18, chans),
        compiler_params=pltpu.CompilerParams(collective_id=0, has_side_effects=True, vmem_limit_bytes=48 << 20),
    )(*args)
    return out.reshape(fr, fc, 2 * flat), grad.reshape(rows, cols, flat), first, upper, second


def solution(mesh):
    in_specs = (P("gx", "gy", None), P(), P(), P(), P(), P(), P("gx", "gy", None), P("gx", "gy"))
    out_specs = (P("gx", "gy", None), P("gx", "gy", None), P(), P(), P())
    return jax.shard_map(
        per_device, mesh=mesh, in_specs=in_specs, out_specs=out_specs, check_vma=False
    )
```

```python
import functools
import math

import jax
import jax.numpy as jnp
from jax import lax
from jax.experimental import pallas as pl
from jax.experimental.pallas import tpu as pltpu
from jax.sharding import PartitionSpec as P


MESH = pl.DeviceIdType.MESH


def add_up(nx, ny, used, part, full, first_in, line, line_in, sems):
    mx, my = lax.axis_index("gx"), lax.axis_index("gy")
    small = part.shape[1] // ny
    s1, r1, s2, r2, s3, r3, s4, r4 = sems

    def piece(i):
        return pl.ds(pl.multiple_of(i * small, 16), small)

    def along_x(d):
        return lax.rem(mx + d, nx)

    def along_y(d):
        return lax.rem(my + d, ny)

    def over_x(pair, send, recv):
        copies = [
            pltpu.make_async_remote_copy(
                src_ref=pair(d)[0], dst_ref=pair(d)[1], send_sem=send.at[d - 1], recv_sem=recv.at[d - 1],
                device_id=(along_x(d), my), device_id_type=MESH)
            for d in range(1, nx)
        ]
        for copy in copies:
            copy.start()
        return copies

    def over_y(pair, send, recv):
        copies = [
            pltpu.make_async_remote_copy(
                src_ref=pair(d)[0], dst_ref=pair(d)[1], send_sem=send.at[d - 1], recv_sem=recv.at[d - 1],
                device_id=(mx, along_y(d)), device_id_type=MESH)
            for d in range(1, ny)
        ]
        for copy in copies:
            copy.start()
        return copies

    copies = over_x(lambda d: (part.at[along_x(d), pl.ds(0, used)], first_in.at[d - 1]), s1, r1)
    yield
    for copy in copies:
        copy.wait()
    total = part[mx, :used, :].astype(jnp.float32)
    for d in range(nx - 1):
        total += first_in[d].astype(jnp.float32)
    line[:used, :] = total.astype(jnp.bfloat16)
    if used < line.shape[0]:
        line[used:, :] = jnp.zeros((line.shape[0] - used, 128), jnp.bfloat16)
    copies = over_y(lambda d: (line.at[piece(along_y(d))], line_in.at[d - 1]), s2, r2)
    yield
    for copy in copies:
        copy.wait()
    total = line[piece(my), :].astype(jnp.float32)
    for d in range(ny - 1):
        total += line_in[d].astype(jnp.float32)
    full[mx, piece(my), :] = total.astype(jnp.bfloat16)
    copies = over_y(lambda d: (full.at[mx, piece(my)], full.at[mx, piece(my)]), s3, r3)
    yield
    for copy in copies:
        copy.wait()
    whole = pl.ds(0, used)
    copies = over_x(lambda d: (full.at[mx, whole], full.at[mx, whole]), s4, r4)
    yield
    for copy in copies:
        copy.wait()


def sum_sizes(nx, ny, blocks, chans):
    used = -(-blocks * chans // (16 * nx)) * 16
    return used, -(-used // (16 * ny)) * 16 * ny


def add_up_scratch(nx, ny, blocks, chans):
    used, chunk = sum_sizes(nx, ny, blocks, chans)
    bf, dma = jnp.bfloat16, pltpu.SemaphoreType.DMA
    return [
        pltpu.VMEM((nx, chunk, 128), bf),
        pltpu.VMEM((nx, chunk, 128), bf),
        pltpu.VMEM((nx - 1, used, 128), bf),
        pltpu.VMEM((chunk, 128), bf),
        pltpu.VMEM((ny - 1, chunk // ny, 128), bf),
        dma((nx - 1,)), dma((nx - 1,)), dma((ny - 1,)), dma((ny - 1,)),
        dma((ny - 1,)), dma((ny - 1,)), dma((nx - 1,)), dma((nx - 1,)),
    ]


def segments(used, start, stop):
    found = []
    while start < stop:
        chunk, row = start // used, start % used
        size = min(used - row, stop - start)
        found.append((chunk, row, size))
        start += size
    return found


def put_block(part, used, block, value):
    at, value = 0, value.astype(jnp.bfloat16)
    height = value.shape[0]
    for chunk, row, size in segments(used, block * height, (block + 1) * height):
        part[chunk, row : row + size, :] = value[at : at + size]
        at += size


def put_taps(part, used, terms):
    wide = part.shape[2]
    for k in range(9):
        put_block(part, used, k, terms[k][:, :wide])
    for j in range(5):
        left = terms[2 * j][:, wide:]
        right = terms[2 * j + 1][:, wide:] if 2 * j + 1 < 9 else jnp.zeros_like(left)
        put_block(part, used, 9 + j, jnp.concatenate([left, right], axis=1))


def clear_end(part, used, rows):
    for chunk, row, size in segments(used, rows, part.shape[0] * used):
        part[chunk, row : row + size, :] = jnp.zeros((size, part.shape[2]), jnp.bfloat16)


def get_block(full, used, block, height):
    pieces = [full[c, r : r + n, :] for c, r, n in segments(used, block * height, (block + 1) * height)]
    return jnp.concatenate(pieces, axis=0).astype(jnp.float32) if len(pieces) > 1 else pieces[0].astype(jnp.float32)


def get_taps(full, used, out):
    chans = out.shape[1]
    for k in range(9):
        out[3 * k : 3 * k + 2] = get_block(full, used, k, chans).T.reshape(2, chans, chans)
    for j in range(5):
        both = get_block(full, used, 9 + j, chans).T
        out[6 * j + 2] = both[:chans]
        if 2 * j + 1 < 9:
            out[6 * j + 5] = both[chans:]


AROUND = [(dx, dy) for dx in (-1, 0, 1) for dy in (-1, 0, 1) if (dx, dy) != (0, 0)]


def act(v, small):
    return 0.2 * v + 0.8 * (jnp.maximum(v, 0.0) + jnp.log(1.0 + small))


def slope(v, small):
    share = 1.0 / (1.0 + small)
    return 0.2 + 0.8 * jnp.where(v >= 0.0, share, small * share)


def leaving(step, size, width):
    return {1: pl.ds(size - width, width), -1: pl.ds(0, width), 0: pl.ds(0, size)}[step]


def landing(step, size, width):
    return {1: pl.ds(0, width), -1: pl.ds(width + size, width), 0: pl.ds(width, size)}[step]


def rim_copies(nx, ny, src, dst, width, send, recv):
    mx, my = lax.axis_index("gx"), lax.axis_index("gy")
    copies = []
    for k, (dx, dy) in enumerate(AROUND):
        part = src.at[leaving(dx, src.shape[0], width), leaving(dy, src.shape[1], width)]
        spot = dst.at[landing(dx, src.shape[0], width), landing(dy, src.shape[1], width)]
        copies.append(pltpu.make_async_remote_copy(
            src_ref=part, dst_ref=spot, send_sem=send.at[k], recv_sem=recv.at[k],
            device_id=(lax.rem(mx + dx + nx, nx), lax.rem(my + dy + ny, ny)), device_id_type=MESH))
    return copies


def shifted(cells):
    flat = cells.reshape((-1,) + cells.shape[-2:])
    depth = flat.shape[1]
    place = lax.broadcasted_iota(jnp.int32, flat.shape, 1)
    lower = jnp.where(place == 0, 0.0, pltpu.roll(flat, 1, 1))
    upper = jnp.where(place == depth - 1, 0.0, pltpu.roll(flat, depth - 1, 1))
    return lower.reshape(cells.shape), upper.reshape(cells.shape)


def coarse_taps(cells):
    cells = cells.astype(jnp.float32)
    lower, upper = shifted(cells)
    return jnp.concatenate([lower, cells, upper], axis=-1).astype(jnp.bfloat16)


def fine_taps(cells):
    lower, upper = shifted(cells)
    lane = lax.broadcasted_iota(jnp.int32, cells.shape, cells.ndim - 1)
    return jnp.where(lane < cells.shape[-1] // 2, upper, lower).astype(jnp.bfloat16)


def times(left, right):
    return jnp.dot(left, right, preferred_element_type=jnp.float32)


def times_t(left, right):
    return lax.dot_general(left, right, (((1,), (1,)), ((), ())), preferred_element_type=jnp.float32)


def conv(taps, weights, rows, cols, product=times):
    total = None
    for k in range(9):
        ox, oy = k // 3, k % 3
        piece = taps[ox : ox + rows, oy : oy + cols]
        piece = piece.reshape(-1, piece.shape[-1])
        term = product(piece, weights[k])
        total = term if total is None else total + term
    return total.reshape(rows, cols, -1, total.shape[1])


def spread_edge(values, axis, inner):
    first, mid, last = values
    shape = list(mid.shape)
    shape[axis] = inner
    return jnp.concatenate([first, jnp.broadcast_to(mid, shape), last], axis=axis)


def block_kernel(nx, ny, fine_scale, coarse_scale, field, cot, w_first, b_first, w_upper, w_second, b_second,
                 out_field, out_grad, out_first, out_upper, out_second,
                 field_ext, cot_ext, ctaps, ftaps, gtaps, rim_ext, rim_out,
                 first_t, up_row, second_n, second_t, s_f, r_f, s_c, r_c, s_g, r_g, *groups):
    mx, my = lax.axis_index("gx"), lax.axis_index("gy")
    rows, cols, depth, wide = field.shape
    chans = wide // 2
    fr, fc = 2 * rows, 2 * cols
    part_a, full_a, *rest_a = groups[: len(groups) // 2]
    part_b, full_b, *rest_b = groups[len(groups) // 2 :]
    used_a, used_b = rest_a[0].shape[1], rest_b[0].shape[1]
    barrier = pltpu.get_barrier_semaphore()
    peers = {((dx + nx) % nx, (dy + ny) % ny) for dx, dy in AROUND}
    peers |= {(d, 0) for d in range(1, nx)} | {(0, d) for d in range(1, ny)}
    for dx, dy in sorted(peers):
        pl.semaphore_signal(barrier, inc=1, device_id=(lax.rem(mx + dx, nx), lax.rem(my + dy, ny)), device_id_type=MESH)
    pl.semaphore_wait(barrier, len(peers))
    field_copies = rim_copies(nx, ny, field, field_ext, 2, s_f, r_f)
    cot_copies = rim_copies(nx, ny, cot, cot_ext, 1, s_c, r_c)
    for copy in field_copies + cot_copies:
        copy.start()
    field_ext[2 : 2 + rows, 2 : 2 + cols] = field[...]
    cot_ext[1 : 1 + fr, 1 : 1 + fc] = cot[...]
    none = jnp.zeros((chans, chans), jnp.bfloat16)
    for k in range(9):
        low, mid, high = w_second[3 * k], w_second[3 * k + 1], w_second[3 * k + 2]
        second_n[k, :chans] = jnp.concatenate([mid, low], axis=1)
        second_n[k, chans : 2 * chans] = jnp.concatenate([high, mid], axis=1)
        second_n[k, 2 * chans : 3 * chans] = jnp.concatenate([none, high], axis=1)
        second_n[k, 3 * chans :] = jnp.concatenate([low, none], axis=1)
        second_t[8 - k, :chans] = jnp.concatenate([mid, low, none, high], axis=1)
        second_t[8 - k, chans:] = jnp.concatenate([high, mid, low, none], axis=1)
        first_t[8 - k] = jnp.concatenate([w_first[3 * k + 2], w_first[3 * k + 1], w_first[3 * k]], axis=1)
    up_row[...] = jnp.concatenate([w_upper[k] for k in range(8)], axis=1)
    for copy in field_copies:
        copy.wait()

    ctaps[...] = coarse_taps(field_ext[..., :chans])
    pre_first = conv(ctaps, w_first[...].reshape(9, 3 * chans, chans), rows + 2, cols + 2) + b_first[...]
    small = jnp.exp(-jnp.abs(pre_first))
    hidden = act(pre_first, small).astype(jnp.bfloat16)
    slope_first = slope(pre_first, small)[1 : 1 + rows, 1 : 1 + cols]
    upper = times(hidden.reshape(-1, chans), up_row[...])
    upper = upper.reshape(rows + 2, cols + 2, depth, 8 * chans)
    sides = []
    for a in (0, 1):
        pair = [upper[..., (2 * a + b) * wide : (2 * a + b + 1) * wide] for b in (0, 1)]
        sides.append(jnp.stack(pair, axis=2).reshape(rows + 2, fc + 4, depth, wide))
    upper = jnp.stack(sides, axis=1).reshape(fr + 4, fc + 4, depth, wide)
    ftaps[..., :wide] = upper.astype(jnp.bfloat16)
    ftaps[..., wide:] = fine_taps(ftaps[..., :wide].astype(jnp.float32))

    pre_second = conv(ftaps, second_n, fr + 2, fc + 2) + b_second[...]
    small = jnp.exp(-jnp.abs(pre_second))
    out_field[...] = act(pre_second, small)[1 : 1 + fr, 1 : 1 + fc].astype(jnp.bfloat16)
    for copy in cot_copies:
        copy.wait()
    ends = ((0, 2, rows + 2), (0, 2, cols + 2))
    bands = []
    for i in ends[0]:
        tiles = [field_ext[i, j, :, chans:].astype(jnp.float32) for j in ends[1]]
        bands.append(spread_edge([jnp.concatenate([t, t], axis=1)[None] for t in tiles], 0, fc)[None])
    weight = spread_edge(bands, 0, fr)
    grad_pre = weight * cot_ext[...].astype(jnp.float32) * slope(pre_second, small)
    gtaps[..., :wide] = grad_pre.astype(jnp.bfloat16)
    gtaps[..., wide:] = fine_taps(gtaps[..., :wide].astype(jnp.float32))

    own_grad = gtaps[1 : 1 + fr, 1 : 1 + fc, :, :wide].reshape(-1, wide)
    own_grad_t = own_grad.astype(jnp.float32).T.astype(jnp.bfloat16)
    terms = []
    for k in range(9):
        ox, oy = 1 + k // 3, 1 + k % 3
        piece = ftaps[ox : ox + fr, oy : oy + fc].reshape(-1, 2 * wide)
        two = times(own_grad_t, piece) * fine_scale
        even, odd = two[:chans], two[chans:]
        tap0 = odd[:, :chans] + even[:, 3 * chans :]
        tap1 = even[:, :chans] + odd[:, chans : 2 * chans]
        tap2 = even[:, chans : 2 * chans] + odd[:, 2 * chans : 3 * chans]
        terms.append(jnp.concatenate([tap0, tap1, tap2], axis=1))
    put_taps(part_a, used_a, terms)
    clear_end(part_a, used_a, 14 * chans)
    sum_a = add_up(nx, ny, used_a, part_a, full_a, *rest_a[:3], rest_a[3:])
    next(sum_a)

    grad_up = conv(gtaps, second_t, fr, fc, times_t).astype(jnp.bfloat16)
    six = grad_up.reshape(rows, 2, cols, 2, depth, wide)
    corner = [six[:, a, :, b].reshape(-1, wide) for a in (0, 1) for b in (0, 1)]
    grad_hidden = times_t(jnp.concatenate(corner, axis=1), up_row[...])
    grad_first = (grad_hidden.reshape(rows, cols, depth, chans) * slope_first).astype(jnp.bfloat16)
    rim_out[...] = jnp.concatenate([grad_first, jnp.zeros_like(grad_first)], axis=-1)
    rim_ext[1 : 1 + rows, 1 : 1 + cols, :, :chans] = grad_first
    rim = rim_copies(nx, ny, rim_out, rim_ext, 1, s_g, r_g)
    for copy in rim:
        copy.start()
    next(sum_a)

    own_hidden = hidden[1 : 1 + rows, 1 : 1 + cols].reshape(-1, chans)
    hidden_t = own_hidden.astype(jnp.float32).T.astype(jnp.bfloat16)
    for k in range(4):
        put_block(part_b, used_b, 14 + k, times(hidden_t, corner[k]) * coarse_scale)
    grad_first_t = grad_first.reshape(-1, chans).astype(jnp.float32).T.astype(jnp.bfloat16)
    terms = []
    for k in range(9):
        ox, oy = 1 + k // 3, 1 + k % 3
        piece = ctaps[ox : ox + rows, oy : oy + cols].reshape(-1, 3 * chans)
        terms.append(times(grad_first_t, piece) * coarse_scale)
    put_taps(part_b, used_b, terms)
    clear_end(part_b, used_b, 18 * chans)
    sum_b = add_up(nx, ny, used_b, part_b, full_b, *rest_b[:3], rest_b[3:])
    next(sum_b)
    next(sum_a)
    for copy in rim:
        copy.wait()
    grad_in = conv(coarse_taps(rim_ext[..., :chans]), first_t, rows, cols, times_t)
    out_grad[...] = grad_in.astype(jnp.bfloat16)
    next(sum_a)
    next(sum_b)
    next(sum_b)
    next(sum_b)
    for _ in sum_a:
        pass
    get_taps(full_a, used_a, out_second)
    for _ in sum_b:
        pass
    get_taps(full_b, used_b, out_first)
    for k in range(4):
        both = get_block(full_b, used_b, 14 + k, chans)
        out_upper[2 * k] = both[:, :chans]
        out_upper[2 * k + 1] = both[:, chans:]


def per_device(field_in, w_first, b_first, w_upper, w_second, b_second, cotangent, tile_weights):
    rows, cols, flat = field_in.shape
    chans = w_first.shape[1]
    depth = flat // chans
    wide = 2 * chans
    nx, ny = lax.axis_size("gx"), lax.axis_size("gy")
    coarse_scale = 1.0 / math.sqrt(rows * cols * depth * nx * ny)
    fine_scale = 1.0 / math.sqrt(8 * rows * cols * depth * nx * ny)
    fr, fc = 2 * rows, 2 * cols
    bf, dma = jnp.bfloat16, pltpu.SemaphoreType.DMA
    cells = field_in.reshape(rows, cols, depth, chans)
    args = (
        jnp.concatenate([cells, jnp.broadcast_to(tile_weights.astype(bf)[..., None, None], cells.shape)], axis=-1),
        cotangent.reshape(fr, fc, depth, wide),
        w_first,
        b_first.reshape(1, chans),
        w_upper,
        w_second,
        jnp.concatenate([b_second, b_second]).reshape(1, wide),
    )
    vmem = pl.BlockSpec(memory_space=pltpu.VMEM)
    out, grad, first, upper, second = pl.pallas_call(
        functools.partial(block_kernel, nx, ny, fine_scale, coarse_scale),
        out_shape=(
            jax.ShapeDtypeStruct((fr, fc, depth, wide), bf),
            jax.ShapeDtypeStruct((rows, cols, depth, chans), bf),
            jax.ShapeDtypeStruct((27, chans, chans), jnp.float32),
            jax.ShapeDtypeStruct((8, chans, chans), jnp.float32),
            jax.ShapeDtypeStruct((27, chans, chans), jnp.float32),
        ),
        in_specs=[vmem] * len(args),
        out_specs=(vmem,) * 5,
        scratch_shapes=[
            pltpu.VMEM((rows + 4, cols + 4, depth, wide), bf),
            pltpu.VMEM((fr + 2, fc + 2, depth, wide), bf),
            pltpu.VMEM((rows + 4, cols + 4, depth, 3 * chans), bf),
            pltpu.VMEM((fr + 4, fc + 4, depth, 2 * wide), bf),
            pltpu.VMEM((fr + 2, fc + 2, depth, 2 * wide), bf),
            pltpu.VMEM((rows + 2, cols + 2, depth, wide), bf),
            pltpu.VMEM((rows, cols, depth, wide), bf),
            pltpu.VMEM((9, chans, 3 * chans), bf),
            pltpu.VMEM((chans, 8 * chans), bf),
            pltpu.VMEM((9, 2 * wide, wide), bf),
            pltpu.VMEM((9, wide, 2 * wide), bf),
        ] + [dma((8,))] * 6 + add_up_scratch(nx, ny, 14, chans) + add_up_scratch(nx, ny, 18, chans),
        compiler_params=pltpu.CompilerParams(collective_id=0, has_side_effects=True, vmem_limit_bytes=48 << 20),
    )(*args)
    return out.reshape(fr, fc, 2 * flat), grad.reshape(rows, cols, flat), first, upper, second


def solution(mesh):
    in_specs = (P("gx", "gy", None), P(), P(), P(), P(), P(), P("gx", "gy", None), P("gx", "gy"))
    out_specs = (P("gx", "gy", None), P("gx", "gy", None), P(), P(), P())
    return jax.shard_map(
        per_device, mesh=mesh, in_specs=in_specs, out_specs=out_specs, check_vma=False
    )
```

```python
import functools
import math

import jax
import jax.numpy as jnp
from jax import lax
from jax.experimental import pallas as pl
from jax.experimental.pallas import tpu as pltpu
from jax.sharding import PartitionSpec as P


MESH = pl.DeviceIdType.MESH


def add_up(nx, ny, used, part, full, first_in, line, line_in, sems):
    mx, my = lax.axis_index("gx"), lax.axis_index("gy")
    small = part.shape[1] // ny
    s1, r1, s2, r2, s3, r3, s4, r4 = sems

    def piece(i):
        return pl.ds(pl.multiple_of(i * small, 16), small)

    def along_x(d):
        return lax.rem(mx + d, nx)

    def along_y(d):
        return lax.rem(my + d, ny)

    def over_x(pair, send, recv):
        copies = [
            pltpu.make_async_remote_copy(
                src_ref=pair(d)[0], dst_ref=pair(d)[1], send_sem=send.at[d - 1], recv_sem=recv.at[d - 1],
                device_id=(along_x(d), my), device_id_type=MESH)
            for d in range(1, nx)
        ]
        for copy in copies:
            copy.start()
        return copies

    def over_y(pair, send, recv):
        copies = [
            pltpu.make_async_remote_copy(
                src_ref=pair(d)[0], dst_ref=pair(d)[1], send_sem=send.at[d - 1], recv_sem=recv.at[d - 1],
                device_id=(mx, along_y(d)), device_id_type=MESH)
            for d in range(1, ny)
        ]
        for copy in copies:
            copy.start()
        return copies

    copies = over_x(lambda d: (part.at[along_x(d), pl.ds(0, used)], first_in.at[d - 1]), s1, r1)
    yield
    for copy in copies:
        copy.wait()
    total = part[mx, :used, :].astype(jnp.float32)
    for d in range(nx - 1):
        total += first_in[d].astype(jnp.float32)
    line[:used, :] = total.astype(jnp.bfloat16)
    if used < line.shape[0]:
        line[used:, :] = jnp.zeros((line.shape[0] - used, 128), jnp.bfloat16)
    copies = over_y(lambda d: (line.at[piece(along_y(d))], line_in.at[d - 1]), s2, r2)
    yield
    for copy in copies:
        copy.wait()
    total = line[piece(my), :].astype(jnp.float32)
    for d in range(ny - 1):
        total += line_in[d].astype(jnp.float32)
    full[mx, piece(my), :] = total.astype(jnp.bfloat16)
    copies = over_y(lambda d: (full.at[mx, piece(my)], full.at[mx, piece(my)]), s3, r3)
    yield
    for copy in copies:
        copy.wait()
    whole = pl.ds(0, used)
    copies = over_x(lambda d: (full.at[mx, whole], full.at[mx, whole]), s4, r4)
    yield
    for copy in copies:
        copy.wait()


def sum_sizes(nx, ny, blocks, chans):
    used = -(-blocks * chans // (16 * nx)) * 16
    return used, -(-used // (16 * ny)) * 16 * ny


def add_up_scratch(nx, ny, blocks, chans):
    used, chunk = sum_sizes(nx, ny, blocks, chans)
    bf, dma = jnp.bfloat16, pltpu.SemaphoreType.DMA
    return [
        pltpu.VMEM((nx, chunk, 128), bf),
        pltpu.VMEM((nx, chunk, 128), bf),
        pltpu.VMEM((nx - 1, used, 128), bf),
        pltpu.VMEM((chunk, 128), bf),
        pltpu.VMEM((ny - 1, chunk // ny, 128), bf),
        dma((nx - 1,)), dma((nx - 1,)), dma((ny - 1,)), dma((ny - 1,)),
        dma((ny - 1,)), dma((ny - 1,)), dma((nx - 1,)), dma((nx - 1,)),
    ]


def segments(used, start, stop):
    found = []
    while start < stop:
        chunk, row = start // used, start % used
        size = min(used - row, stop - start)
        found.append((chunk, row, size))
        start += size
    return found


def put_block(part, used, block, value):
    at, value = 0, value.astype(jnp.bfloat16)
    height = value.shape[0]
    for chunk, row, size in segments(used, block * height, (block + 1) * height):
        part[chunk, row : row + size, :] = value[at : at + size]
        at += size


def put_taps(part, used, terms):
    wide = part.shape[2]
    for k in range(9):
        put_block(part, used, k, terms[k][:, :wide])
    for j in range(5):
        left = terms[2 * j][:, wide:]
        right = terms[2 * j + 1][:, wide:] if 2 * j + 1 < 9 else jnp.zeros_like(left)
        put_block(part, used, 9 + j, jnp.concatenate([left, right], axis=1))


def clear_end(part, used, rows):
    for chunk, row, size in segments(used, rows, part.shape[0] * used):
        part[chunk, row : row + size, :] = jnp.zeros((size, part.shape[2]), jnp.bfloat16)


def get_block(full, used, block, height):
    pieces = [full[c, r : r + n, :] for c, r, n in segments(used, block * height, (block + 1) * height)]
    return jnp.concatenate(pieces, axis=0).astype(jnp.float32) if len(pieces) > 1 else pieces[0].astype(jnp.float32)


def get_taps(full, used, out):
    chans = out.shape[1]
    for k in range(9):
        out[3 * k : 3 * k + 2] = get_block(full, used, k, chans).T.reshape(2, chans, chans)
    for j in range(5):
        both = get_block(full, used, 9 + j, chans).T
        out[6 * j + 2] = both[:chans]
        if 2 * j + 1 < 9:
            out[6 * j + 5] = both[chans:]


AROUND = [(dx, dy) for dx in (-1, 0, 1) for dy in (-1, 0, 1) if (dx, dy) != (0, 0)]


def act(v, small):
    return 0.2 * v + 0.8 * (jnp.maximum(v, 0.0) + jnp.log(1.0 + small))


def slope(v, small):
    share = 1.0 / (1.0 + small)
    return 0.2 + 0.8 * jnp.where(v >= 0.0, share, small * share)


def leaving(step, size, width):
    return {1: pl.ds(size - width, width), -1: pl.ds(0, width), 0: pl.ds(0, size)}[step]


def landing(step, size, width):
    return {1: pl.ds(0, width), -1: pl.ds(width + size, width), 0: pl.ds(width, size)}[step]


def rim_copies(nx, ny, src, dst, width, send, recv):
    mx, my = lax.axis_index("gx"), lax.axis_index("gy")
    copies = []
    for k, (dx, dy) in enumerate(AROUND):
        part = src.at[leaving(dx, src.shape[0], width), leaving(dy, src.shape[1], width)]
        spot = dst.at[landing(dx, src.shape[0], width), landing(dy, src.shape[1], width)]
        copies.append(pltpu.make_async_remote_copy(
            src_ref=part, dst_ref=spot, send_sem=send.at[k], recv_sem=recv.at[k],
            device_id=(lax.rem(mx + dx + nx, nx), lax.rem(my + dy + ny, ny)), device_id_type=MESH))
    return copies


def shifted(cells):
    flat = cells.reshape((-1,) + cells.shape[-2:])
    depth = flat.shape[1]
    place = lax.broadcasted_iota(jnp.int32, flat.shape, 1)
    lower = jnp.where(place == 0, 0.0, pltpu.roll(flat, 1, 1))
    upper = jnp.where(place == depth - 1, 0.0, pltpu.roll(flat, depth - 1, 1))
    return lower.reshape(cells.shape), upper.reshape(cells.shape)


def coarse_taps(cells):
    cells = cells.astype(jnp.float32)
    lower, upper = shifted(cells)
    return jnp.concatenate([lower, cells, upper], axis=-1).astype(jnp.bfloat16)


def fine_taps(cells):
    lower, upper = shifted(cells)
    lane = lax.broadcasted_iota(jnp.int32, cells.shape, cells.ndim - 1)
    return jnp.where(lane < cells.shape[-1] // 2, upper, lower).astype(jnp.bfloat16)


def times(left, right):
    return jnp.dot(left, right, preferred_element_type=jnp.float32)


def times_t(left, right):
    return lax.dot_general(left, right, (((1,), (1,)), ((), ())), preferred_element_type=jnp.float32)


def conv(taps, weights, rows, cols, product=times):
    total = None
    for k in range(9):
        ox, oy = k // 3, k % 3
        piece = taps[ox : ox + rows, oy : oy + cols]
        piece = piece.reshape(-1, piece.shape[-1])
        term = product(piece, weights[k])
        total = term if total is None else total + term
    return total.reshape(rows, cols, -1, total.shape[1])


def spread_edge(values, axis, inner):
    first, mid, last = values
    shape = list(mid.shape)
    shape[axis] = inner
    return jnp.concatenate([first, jnp.broadcast_to(mid, shape), last], axis=axis)


def block_kernel(nx, ny, fine_scale, coarse_scale, field, cot, w_first, b_first, w_upper, w_second, b_second,
                 out_field, out_grad, out_first, out_upper, out_second,
                 field_ext, cot_ext, ctaps, ftaps, gtaps, rim_ext, rim_out,
                 first_t, up_row, second_n, second_t, s_f, r_f, s_c, r_c, s_g, r_g, *groups):
    mx, my = lax.axis_index("gx"), lax.axis_index("gy")
    rows, cols, depth, wide = field.shape
    chans = wide // 2
    fr, fc = 2 * rows, 2 * cols
    part_a, full_a, *rest_a = groups[: len(groups) // 2]
    part_b, full_b, *rest_b = groups[len(groups) // 2 :]
    used_a, used_b = rest_a[0].shape[1], rest_b[0].shape[1]
    barrier = pltpu.get_barrier_semaphore()
    peers = {((dx + nx) % nx, (dy + ny) % ny) for dx, dy in AROUND}
    peers |= {(d, 0) for d in range(1, nx)} | {(0, d) for d in range(1, ny)}
    for dx, dy in sorted(peers):
        pl.semaphore_signal(barrier, inc=1, device_id=(lax.rem(mx + dx, nx), lax.rem(my + dy, ny)), device_id_type=MESH)
    pl.semaphore_wait(barrier, len(peers))
    field_copies = rim_copies(nx, ny, field, field_ext, 2, s_f, r_f)
    cot_copies = rim_copies(nx, ny, cot, cot_ext, 1, s_c, r_c)
    for copy in field_copies + cot_copies:
        copy.start()
    field_ext[2 : 2 + rows, 2 : 2 + cols] = field[...]
    cot_ext[1 : 1 + fr, 1 : 1 + fc] = cot[...]
    none = jnp.zeros((chans, chans), jnp.bfloat16)
    for k in range(9):
        low, mid, high = w_second[3 * k], w_second[3 * k + 1], w_second[3 * k + 2]
        second_n[k, :chans] = jnp.concatenate([mid, low], axis=1)
        second_n[k, chans : 2 * chans] = jnp.concatenate([high, mid], axis=1)
        second_n[k, 2 * chans : 3 * chans] = jnp.concatenate([none, high], axis=1)
        second_n[k, 3 * chans :] = jnp.concatenate([low, none], axis=1)
        second_t[8 - k, :chans] = jnp.concatenate([mid, low, none, high], axis=1)
        second_t[8 - k, chans:] = jnp.concatenate([high, mid, low, none], axis=1)
        first_t[8 - k] = jnp.concatenate([w_first[3 * k + 2], w_first[3 * k + 1], w_first[3 * k]], axis=1)
    up_row[...] = jnp.concatenate([w_upper[k] for k in range(8)], axis=1)
    for copy in field_copies:
        copy.wait()

    ctaps[...] = coarse_taps(field_ext[..., :chans])
    pre_first = conv(ctaps, w_first[...].reshape(9, 3 * chans, chans), rows + 2, cols + 2) + b_first[...]
    small = jnp.exp(-jnp.abs(pre_first))
    hidden = act(pre_first, small).astype(jnp.bfloat16)
    slope_first = slope(pre_first, small)[1 : 1 + rows, 1 : 1 + cols]
    upper = times(hidden.reshape(-1, chans), up_row[...])
    upper = upper.reshape(rows + 2, cols + 2, depth, 8 * chans)
    sides = []
    for a in (0, 1):
        pair = [upper[..., (2 * a + b) * wide : (2 * a + b + 1) * wide] for b in (0, 1)]
        sides.append(jnp.stack(pair, axis=2).reshape(rows + 2, fc + 4, depth, wide))
    upper = jnp.stack(sides, axis=1).reshape(fr + 4, fc + 4, depth, wide)
    ftaps[..., :wide] = upper.astype(jnp.bfloat16)
    ftaps[..., wide:] = fine_taps(ftaps[..., :wide].astype(jnp.float32))

    pre_second = conv(ftaps, second_n, fr + 2, fc + 2) + jnp.concatenate([b_second[...], b_second[...]], axis=1)
    small = jnp.exp(-jnp.abs(pre_second))
    out_field[...] = act(pre_second, small)[1 : 1 + fr, 1 : 1 + fc].astype(jnp.bfloat16)
    for copy in cot_copies:
        copy.wait()
    ends = ((0, 2, rows + 2), (0, 2, cols + 2))
    bands = []
    for i in ends[0]:
        tiles = [field_ext[i, j, :, chans:].astype(jnp.float32) for j in ends[1]]
        bands.append(spread_edge([jnp.concatenate([t, t], axis=1)[None] for t in tiles], 0, fc)[None])
    weight = spread_edge(bands, 0, fr)
    grad_pre = weight * cot_ext[...].astype(jnp.float32) * slope(pre_second, small)
    gtaps[..., :wide] = grad_pre.astype(jnp.bfloat16)
    gtaps[..., wide:] = fine_taps(gtaps[..., :wide].astype(jnp.float32))

    own_grad = gtaps[1 : 1 + fr, 1 : 1 + fc, :, :wide].reshape(-1, wide)
    own_grad_t = own_grad.astype(jnp.float32).T.astype(jnp.bfloat16)
    terms = []
    for k in range(9):
        ox, oy = 1 + k // 3, 1 + k % 3
        piece = ftaps[ox : ox + fr, oy : oy + fc].reshape(-1, 2 * wide)
        two = times(own_grad_t, piece) * fine_scale
        even, odd = two[:chans], two[chans:]
        tap0 = odd[:, :chans] + even[:, 3 * chans :]
        tap1 = even[:, :chans] + odd[:, chans : 2 * chans]
        tap2 = even[:, chans : 2 * chans] + odd[:, 2 * chans : 3 * chans]
        terms.append(jnp.concatenate([tap0, tap1, tap2], axis=1))
    put_taps(part_a, used_a, terms)
    clear_end(part_a, used_a, 14 * chans)
    sum_a = add_up(nx, ny, used_a, part_a, full_a, *rest_a[:3], rest_a[3:])
    next(sum_a)

    grad_up = conv(gtaps, second_t, fr, fc, times_t).astype(jnp.bfloat16)
    six = grad_up.reshape(rows, 2, cols, 2, depth, wide)
    corner = [six[:, a, :, b].reshape(-1, wide) for a in (0, 1) for b in (0, 1)]
    grad_hidden = times_t(jnp.concatenate(corner, axis=1), up_row[...])
    grad_first = (grad_hidden.reshape(rows, cols, depth, chans) * slope_first).astype(jnp.bfloat16)
    rim_out[...] = jnp.concatenate([grad_first, jnp.zeros_like(grad_first)], axis=-1)
    rim_ext[1 : 1 + rows, 1 : 1 + cols, :, :chans] = grad_first
    rim = rim_copies(nx, ny, rim_out, rim_ext, 1, s_g, r_g)
    for copy in rim:
        copy.start()
    next(sum_a)

    own_hidden = hidden[1 : 1 + rows, 1 : 1 + cols].reshape(-1, chans)
    hidden_t = own_hidden.astype(jnp.float32).T.astype(jnp.bfloat16)
    for k in range(4):
        put_block(part_b, used_b, 14 + k, times(hidden_t, corner[k]) * coarse_scale)
    grad_first_t = grad_first.reshape(-1, chans).astype(jnp.float32).T.astype(jnp.bfloat16)
    terms = []
    for k in range(9):
        ox, oy = 1 + k // 3, 1 + k % 3
        piece = ctaps[ox : ox + rows, oy : oy + cols].reshape(-1, 3 * chans)
        terms.append(times(grad_first_t, piece) * coarse_scale)
    put_taps(part_b, used_b, terms)
    clear_end(part_b, used_b, 18 * chans)
    sum_b = add_up(nx, ny, used_b, part_b, full_b, *rest_b[:3], rest_b[3:])
    next(sum_b)
    next(sum_a)
    for copy in rim:
        copy.wait()
    grad_in = conv(coarse_taps(rim_ext[..., :chans]), first_t, rows, cols, times_t)
    out_grad[...] = grad_in.astype(jnp.bfloat16)
    next(sum_a)
    next(sum_b)
    next(sum_b)
    next(sum_b)
    for _ in sum_a:
        pass
    get_taps(full_a, used_a, out_second)
    for _ in sum_b:
        pass
    get_taps(full_b, used_b, out_first)
    for k in range(4):
        both = get_block(full_b, used_b, 14 + k, chans)
        out_upper[2 * k] = both[:, :chans]
        out_upper[2 * k + 1] = both[:, chans:]


def per_device(field_in, w_first, b_first, w_upper, w_second, b_second, cotangent, tile_weights):
    rows, cols, flat = field_in.shape
    chans = w_first.shape[1]
    depth = flat // chans
    wide = 2 * chans
    nx, ny = lax.axis_size("gx"), lax.axis_size("gy")
    coarse_scale = 1.0 / math.sqrt(rows * cols * depth * nx * ny)
    fine_scale = 1.0 / math.sqrt(8 * rows * cols * depth * nx * ny)
    fr, fc = 2 * rows, 2 * cols
    bf, dma = jnp.bfloat16, pltpu.SemaphoreType.DMA
    cells = field_in.reshape(rows, cols, depth, chans)
    args = (
        jnp.concatenate([cells, jnp.broadcast_to(tile_weights.astype(bf)[..., None, None], cells.shape)], axis=-1),
        cotangent.reshape(fr, fc, depth, wide),
        w_first,
        b_first.reshape(1, chans),
        w_upper,
        w_second,
        b_second.reshape(1, chans),
    )
    vmem = pl.BlockSpec(memory_space=pltpu.VMEM)
    out, grad, first, upper, second = pl.pallas_call(
        functools.partial(block_kernel, nx, ny, fine_scale, coarse_scale),
        out_shape=(
            jax.ShapeDtypeStruct((fr, fc, depth, wide), bf),
            jax.ShapeDtypeStruct((rows, cols, depth, chans), bf),
            jax.ShapeDtypeStruct((27, chans, chans), jnp.float32),
            jax.ShapeDtypeStruct((8, chans, chans), jnp.float32),
            jax.ShapeDtypeStruct((27, chans, chans), jnp.float32),
        ),
        in_specs=[vmem] * len(args),
        out_specs=(vmem,) * 5,
        scratch_shapes=[
            pltpu.VMEM((rows + 4, cols + 4, depth, wide), bf),
            pltpu.VMEM((fr + 2, fc + 2, depth, wide), bf),
            pltpu.VMEM((rows + 4, cols + 4, depth, 3 * chans), bf),
            pltpu.VMEM((fr + 4, fc + 4, depth, 2 * wide), bf),
            pltpu.VMEM((fr + 2, fc + 2, depth, 2 * wide), bf),
            pltpu.VMEM((rows + 2, cols + 2, depth, wide), bf),
            pltpu.VMEM((rows, cols, depth, wide), bf),
            pltpu.VMEM((9, chans, 3 * chans), bf),
            pltpu.VMEM((chans, 8 * chans), bf),
            pltpu.VMEM((9, 2 * wide, wide), bf),
            pltpu.VMEM((9, wide, 2 * wide), bf),
        ] + [dma((8,))] * 6 + add_up_scratch(nx, ny, 14, chans) + add_up_scratch(nx, ny, 18, chans),
        compiler_params=pltpu.CompilerParams(collective_id=0, has_side_effects=True, vmem_limit_bytes=48 << 20),
    )(*args)
    return out.reshape(fr, fc, 2 * flat), grad.reshape(rows, cols, flat), first, upper, second


def solution(mesh):
    in_specs = (P("gx", "gy", None), P(), P(), P(), P(), P(), P("gx", "gy", None), P("gx", "gy"))
    out_specs = (P("gx", "gy", None), P("gx", "gy", None), P(), P(), P())
    return jax.shard_map(
        per_device, mesh=mesh, in_specs=in_specs, out_specs=out_specs, check_vma=False
    )
```
